32 devices in a mesh: groups: 2 (over y), dp: 4 (over z), mp: 2 (over x), pipe: 2 (over core).
Axes of the slice: x: 2, y: 2, z: 4, core: 2. Of those that a mesh axis runs over, the one named last changes fastest.
Arguments:
- tokens: bfloat16 [16384, 4608], P(('groups', 'dp', 'pipe'), 'mp'), parts along dimension 0, may hold values from -6 to 6
- cotangent: bfloat16 [16384, 2048], P(('groups', 'dp', 'pipe'), 'mp'), parts along dimension 0, may hold values from -0.15625 to 0.15625
- tok_job: int32 [16384], P(('groups', 'dp', 'pipe')), parts along dimension 0, may hold values from 0 to 3, as said below
- job_list: int32 [8, 2, 2], P('groups'), parts along dimension 0, may hold values from 0 to 3, as said below
- job_rank: int32 [8], P('groups'), parts along dimension 0, may hold values from 16 to 128, as said below
- adapter_a: bfloat16 [8, 128, 4608], P('groups', 'dp', 'mp'), parts along dimension 0, may hold values from -0.09375 to 0.09375
- adapter_b: bfloat16 [8, 128, 2048], P('groups', 'dp', 'mp'), parts along dimension 0, may hold values from -0.5 to 0.5
Outputs:
- adapted: bfloat16 [16384, 2048], P(('groups', 'dp', 'pipe'), 'mp'), parts along dimension 0
- grad_a: float32 [8, 128, 4608], P('groups', ('dp', 'pipe'), 'mp'), parts along dimension 0
- grad_b: float32 [8, 128, 2048], P('groups', ('dp', 'pipe'), 'mp'), parts along dimension 0
The draws below stay inside these ranges and needn't reach their ends.
There are 2 independent parts, one for each index of `groups`. The reference program is written for one: setup_inputs(seed, part) draws one part's arguments, and reference() takes and returns one part's arrays. A program takes and returns all parts, laid end to end along the dimension named above; each array names one. Nothing has to cross between parts.
Inputs may be any that keep to these rules, and one draw needn't show every extreme that they name: `tok_job`: the tokens of device block b, rows b * 1024 to (b + 1) * 1024 - 1 with b = dp index * 2 + pipe index, have jobs from that device's entry of job_list. `job_list`: each device's 2 jobs are distinct. `job_rank`: every rank is a multiple of 16.
All inputs are finite; a program needn't handle non-finite values.
Results may differ from the reference program's by a relative error of at most 0.005.
Values may be sent and summed in bfloat16 or wider, within the bound.
A program may use at most 64 MiB of HBM per device.

```python
import jax
import jax.numpy as jnp
from jax import lax

D = 4608
O = 2048
R = 128
ACT = 4
JOBS_DEV = 2
TOK_DEV = 1024
TOKENS = 8192
N_DP = 4
N_PIPE = 2


def shared_lists(key):
    base = jax.random.fold_in(key, 11)
    keys = jax.random.split(base, N_DP * N_PIPE)
    orders = jax.vmap(lambda single: jax.random.permutation(single, ACT))(keys)
    return orders[:, :JOBS_DEV].astype(jnp.int32)


def draw_job_list(key, part):
    anchor = key
    lists = shared_lists(anchor)
    return lists.reshape(N_DP, N_PIPE, JOBS_DEV)


def draw_tok_job(key, part):
    anchor = key
    key = jax.random.fold_in(key, 5)
    lists = shared_lists(anchor)
    picks = jax.random.randint(key, (N_DP * N_PIPE, TOK_DEV), 0, JOBS_DEV)
    chosen = jnp.take_along_axis(lists, picks, axis=1)
    return chosen.reshape(N_DP * N_PIPE * TOK_DEV).astype(jnp.int32)


def draw_job_rank(key, part):
    key = jax.random.fold_in(key, 7)
    first, second = jax.random.split(key)
    order = jax.random.permutation(first, ACT)
    steps = jax.random.randint(second, (ACT,), 1, 9)
    steps = jnp.where(order == 0, 8, jnp.where(order == 1, 1, steps))
    return (steps * (R // 8)).astype(jnp.int32)


def steps_of(own_key, dims, cuts, smallest, high):
    def one(axis_at, blocks):
        steps = jax.random.uniform(jax.random.fold_in(jax.random.fold_in(own_key, 6), axis_at), (blocks,), jnp.float32, smallest / len(cuts), high / len(cuts))
        return jnp.repeat(jnp.exp(steps), dims[axis_at] // blocks).reshape((-1,) + (1,) * (len(dims) - axis_at - 1))

    loudness = one(*cuts[0])
    for cut in cuts[1:]:
        loudness = loudness * one(*cut)
    return loudness


def normal_values(key, shape, deviation, most, shards=(), kind=jnp.bfloat16):
    loudness = steps_of(key, shape, shards, -0.22, 0.18) if shards else 1.0
    drawn = jax.random.normal(key, shape, jnp.float32) * deviation * loudness
    return jnp.minimum(jnp.maximum(drawn, -most), most).astype(kind)


def setup_inputs(seed: int = 0, part: int = 0) -> dict:
    splits = jax.random.split(jax.random.key(seed), 8)
    own_keys = jax.random.split(jax.random.fold_in(splits[7], part), 8)
    tokens = normal_values(own_keys[0], (TOKENS, D), 1.0, 6.0, ((0, 8), (1, 2)))
    cotangent = normal_values(own_keys[1], (TOKENS, O), (TOKENS ** -0.5), 0.15625, ((0, 8), (1, 2)))
    tok_job = draw_tok_job(jax.random.fold_in(jax.random.fold_in(splits[7], part), 71), part)
    job_list = draw_job_list(jax.random.fold_in(jax.random.fold_in(splits[7], part), 71), part)
    job_rank = draw_job_rank(jax.random.fold_in(jax.random.fold_in(splits[7], part), 71), part)
    adapter_a = normal_values(own_keys[5], (ACT, R, D), D ** -0.5, 0.09375, ((1, 4), (2, 2)))
    adapter_b = normal_values(own_keys[6], (ACT, R, O), R ** -0.5, 0.5, ((1, 4), (2, 2)))
    return dict(tokens=tokens, cotangent=cotangent, tok_job=tok_job, job_list=job_list, job_rank=job_rank, adapter_a=adapter_a, adapter_b=adapter_b)


def reference(tokens, cotangent, tok_job, job_list, job_rank, adapter_a, adapter_b):
    blocks = N_DP * N_PIPE
    width_o = cotangent.shape[1]
    feats = tokens.reshape(blocks, TOK_DEV, D)
    grads = cotangent.reshape(blocks, TOK_DEV, width_o)
    job_rows = tok_job.reshape(blocks, TOK_DEV)
    lists = job_list.reshape(blocks, JOBS_DEV)
    levels = jnp.arange(R, dtype=jnp.int32)
    everyone = jnp.arange(ACT, dtype=jnp.int32)
    high = lax.Precision.HIGHEST

    def one_block(carry, item):
        grad_a, grad_b = carry
        block_x, block_dy, block_jobs, block_list = item
        onehot = (block_jobs[:, None] == block_list[None, :]).astype(jnp.float32)
        tiles_a = adapter_a[block_list].astype(jnp.float32)
        tiles_b = adapter_b[block_list].astype(jnp.float32)
        slot_ranks = job_rank[block_list]
        slot_mask = (levels[None, :] < slot_ranks[:, None]).astype(jnp.float32)
        slot_scale = 8.0 / jnp.sqrt(slot_ranks.astype(jnp.float32))
        tok_mask = jnp.dot(onehot, slot_mask, precision=high)
        tok_scale = jnp.dot(onehot, slot_scale, precision=high)
        low_all = jnp.einsum('td,jrd->tjr', block_x.astype(jnp.float32), tiles_a, precision=high)
        back_all = jnp.einsum('to,jro->tjr', block_dy.astype(jnp.float32), tiles_b, precision=high)
        low = lax.optimization_barrier(jnp.sum(onehot[:, :, None] * low_all, axis=1))
        back = lax.optimization_barrier(jnp.sum(onehot[:, :, None] * back_all, axis=1))
        scaled_low = (low * tok_mask * tok_scale[:, None]).astype(jnp.bfloat16).astype(jnp.float32)
        scaled_back = (back * tok_mask * tok_scale[:, None]).astype(jnp.bfloat16).astype(jnp.float32)
        spread_low = onehot[:, :, None] * scaled_low[:, None, :]
        spread_back = onehot[:, :, None] * scaled_back[:, None, :]
        adapted = jnp.einsum('tjr,jro->to', spread_low, tiles_b, precision=high).astype(jnp.bfloat16)
        part_b = jnp.einsum('tjr,to->jro', spread_low, block_dy.astype(jnp.float32), precision=high)
        part_a = jnp.einsum('tjr,td->jrd', spread_back, block_x.astype(jnp.float32), precision=high)
        select = (block_list[:, None] == everyone[None, :]).astype(jnp.float32)
        grad_a = grad_a + jnp.einsum('ja,jrd->ard', select, part_a, precision=high)
        grad_b = grad_b + jnp.einsum('ja,jro->aro', select, part_b, precision=high)
        return ((grad_a, grad_b), adapted)
    start = (jnp.zeros((ACT, R, D), jnp.float32), jnp.zeros((ACT, R, width_o), jnp.float32))
    (grad_a, grad_b), adapted = lax.scan(one_block, start, (feats, grads, job_rows, lists))
    return (adapted.reshape(blocks * TOK_DEV, width_o), grad_a, grad_b)
```

```python
import functools

import jax
import jax.numpy as jnp
from jax import lax
from jax.experimental import pallas as pl
from jax.experimental.pallas import tpu as pltpu
from jax.sharding import PartitionSpec as P

TILE = 256
ROWS16 = 16
MESH = pl.DeviceIdType.MESH
NT = (((1,), (1,)), ((), ()))
TN = (((0,), (0,)), ((), ()))


def fused(n, pipes, mps,
          tokens_hbm, cot_hbm, job_ref, list_ref, rank_ref, a_hbm, b_hbm,
          adapted, grad_a, grad_b,
          tokens, cot, all_a, all_b, own, away, here_mp, spread, flat_b,
          part_a, part_b, got_a, got_b,
          local_sem, right_sem, left_sem, line_sem, sib_send, sib_recv,
          mp_send, mp_recv, rs_send, rs_recv):
    z = lax.axis_index("dp")
    core = lax.axis_index("pipe")
    lane = lax.axis_index("mp")
    me = z * pipes + core
    adapters, slots_here = a_hbm.shape[0], a_hbm.shape[1]
    count = tokens.shape[0]
    rank_full = n * slots_here
    half = adapters // pipes
    team = n * pipes

    loads = [
        pltpu.make_async_copy(b_hbm, all_b.at[z], local_sem.at[0]),
        pltpu.make_async_copy(cot_hbm, cot, local_sem.at[1]),
        pltpu.make_async_copy(a_hbm, all_a.at[z], local_sem.at[2]),
        pltpu.make_async_copy(tokens_hbm, tokens, local_sem.at[3]),
    ]
    for load in loads:
        load.start()

    barrier = pltpu.get_barrier_semaphore()
    for step in range(1, team):
        peer = lax.rem(me + step, team)
        pl.semaphore_signal(barrier, inc=1, device_id={"dp": peer // pipes, "pipe": lax.rem(peer, pipes)}, device_id_type=MESH)
    for step in range(1, mps):
        pl.semaphore_signal(barrier, inc=1, device_id={"mp": lax.rem(lane + step, mps)}, device_id_type=MESH)
    pl.semaphore_wait(barrier, team - 1 + mps - 1)

    stores = (all_a, all_b)
    sources = (a_hbm, b_hbm)

    def part_of(ref, c):
        return ref.at[pl.ds(c * half, half)]

    def line_copy(which, shard, rightward, first):
        held = stores[which]
        src = part_of(sources[which], core) if first else part_of(held.at[shard], core)
        sem = right_sem if rightward else left_sem
        return pltpu.make_async_remote_copy(
            src_ref=src, dst_ref=part_of(held.at[shard], core),
            send_sem=sem.at[which, shard], recv_sem=line_sem.at[which, shard],
            device_id={"dp": z + 1 if rightward else z - 1}, device_id_type=MESH)

    def sib_copy(which, shard, c):
        held = stores[which]
        return pltpu.make_async_remote_copy(
            src_ref=part_of(held.at[shard], c), dst_ref=part_of(held.at[shard], c),
            send_sem=sib_send.at[which, shard], recv_sem=sib_recv.at[which, shard],
            device_id={"pipe": 1 - core}, device_id_type=MESH)

    near = jnp.minimum(z, n - 1 - z)

    def shard_at(i):
        if i == 0:
            return z
        paired = z - (i + 1) // 2 if i % 2 else z + i // 2
        return jnp.where(i <= 2 * near, paired, jnp.where(z < n - 1 - z, i, n - 1 - i))

    def send_first(which):
        @pl.when(z < n - 1)
        def _():
            line_copy(which, z, True, True).start()

        @pl.when(z > 0)
        def _():
            line_copy(which, z, False, True).start()

    def forward(which, i):
        shard = shard_at(i)
        line_copy(which, shard, True, False).wait_recv()

        @pl.when(jnp.logical_and(shard < z, z < n - 1))
        def _():
            line_copy(which, shard, True, False).start()

        @pl.when(jnp.logical_and(shard > z, z > 0))
        def _():
            line_copy(which, shard, False, False).start()

        sib_copy(which, shard, core).start()

    def finish_sends(which):
        for i in range(n):
            shard = shard_at(i)

            @pl.when(jnp.logical_and(shard <= z, z < n - 1))
            def _():
                line_copy(which, shard, True, i == 0).wait_send()

            @pl.when(jnp.logical_and(shard >= z, z > 0))
            def _():
                line_copy(which, shard, False, i == 0).wait_send()

            if i > 0:
                sib_copy(which, shard, core).wait_send()

    def mp_copy(which, shard, step):
        return pltpu.make_async_remote_copy(
            src_ref=away.at[which, shard], dst_ref=here_mp.at[which, lane, shard],
            send_sem=mp_send.at[which, shard, step], recv_sem=mp_recv.at[which, lane, shard],
            device_id={"mp": lax.rem(lane + step, mps)}, device_id_type=MESH)

    def mp_arrived(which, shard, step):
        peer = lax.rem(lane + step, mps)
        return pltpu.make_async_remote_copy(
            src_ref=away.at[which, shard], dst_ref=here_mp.at[which, peer, shard],
            send_sem=mp_send.at[which, shard, step], recv_sem=mp_recv.at[which, peer, shard],
            device_id={"mp": peer}, device_id_type=MESH)

    def project(which, i):
        shard = shard_at(i)
        held = stores[which]
        rows = tokens if which == 0 else cot
        if i > 0:
            sib_copy(which, shard, 1 - core).wait_recv()
        factor = held[shard].reshape(adapters * slots_here, held.shape[3])

        @pl.loop(0, count // TILE)
        def _(tile):
            cols = pl.ds(pl.multiple_of(tile * TILE, TILE), TILE)
            got = lax.dot_general(factor, rows[cols, :], NT, preferred_element_type=jnp.float32)
            jobs = job_ref[:, cols]
            value = jnp.zeros((slots_here, TILE), jnp.float32)
            for a in range(adapters):
                value = jnp.where(jobs == a, got[a * slots_here:(a + 1) * slots_here], value)
            own[which, shard, :, cols] = value
            away[which, shard, :, cols] = value.astype(jnp.bfloat16)

        for step in range(1, mps):
            mp_copy(which, shard, step).start()

    first_job = list_ref[z, core, 0]
    second_job = list_ref[z, core, 1]

    def scale(which):
        jobs = job_ref[...]
        ranks = jnp.zeros_like(jobs)
        for a in range(adapters):
            ranks = jnp.where(jobs == a, rank_ref[a], ranks)
        gain = 8.0 / jnp.sqrt(ranks.astype(jnp.float32))
        for shard in range(n):
            value = own[which, shard]
            for step in range(1, mps):
                mp_arrived(which, shard, step).wait_recv()
                value = value + here_mp[which, lax.rem(lane + step, mps), shard].astype(jnp.float32)
            level = lax.broadcasted_iota(jnp.int32, value.shape, 0) + shard * slots_here
            value = jnp.where(level < ranks, value * gain, 0.0)
            base = shard * slots_here
            spread[which, base:base + slots_here, :] = jnp.where(jobs == first_job, value, 0.0).astype(jnp.bfloat16)
            base += rank_full
            spread[which, base:base + slots_here, :] = jnp.where(jobs == second_job, value, 0.0).astype(jnp.bfloat16)

    def rs_copy(which, step):
        dest = lax.rem(me + step, team)
        part, got = ((part_a, got_a), (part_b, got_b))[which]
        return pltpu.make_async_remote_copy(
            src_ref=part.at[dest], dst_ref=got.at[me],
            send_sem=rs_send.at[which, step], recv_sem=rs_recv.at[which, me],
            device_id={"dp": dest // pipes, "pipe": lax.rem(dest, pipes)}, device_id_type=MESH)

    def rs_arrived(which, step):
        src = lax.rem(me + step, team)
        part, got = ((part_a, got_a), (part_b, got_b))[which]
        return pltpu.make_async_remote_copy(
            src_ref=part.at[src], dst_ref=got.at[src],
            send_sem=rs_send.at[which, step], recv_sem=rs_recv.at[which, src],
            device_id={"dp": src // pipes, "pipe": lax.rem(src, pipes)}, device_id_type=MESH)

    far_first = sorted(range(1, team), key=lambda step: abs(step - team // 2))

    def gradient(which):
        rows = tokens if which == 0 else cot
        part, got = ((part_a, got_a), (part_b, got_b))[which]
        weights = spread[1 - which]
        each = rank_full // team

        @pl.loop(0, rows.shape[1] // TILE)
        def _(tile):
            cols = pl.ds(pl.multiple_of(tile * TILE, TILE), TILE)
            out = jnp.dot(weights, rows[:, cols], preferred_element_type=jnp.float32).astype(jnp.bfloat16)
            for dest in range(team):
                for slot in range(2):
                    base = slot * rank_full + dest * each
                    part[dest, slot, :, cols] = out[base:base + each]

        for step in far_first:
            rs_copy(which, step).start()
        got[me] = part[me]

    def collect(which):
        part, got = ((part_a, got_a), (part_b, got_b))[which]
        out = (grad_a, grad_b)[which]
        for step in range(1, team):
            rs_arrived(which, step).wait_recv()

        @pl.loop(0, out.shape[2] // TILE)
        def _(tile):
            cols = pl.ds(pl.multiple_of(tile * TILE, TILE), TILE)
            sums = [jnp.zeros((out.shape[1], TILE), jnp.float32) for _ in range(adapters)]
            for src in range(team):
                for slot in range(2):
                    job = list_ref[src // pipes, src % pipes, slot]
                    term = got[src, slot, :, cols].astype(jnp.float32)
                    for a in range(adapters):
                        sums[a] = sums[a] + term * jnp.where(job == a, 1.0, 0.0)
            for a in range(adapters):
                out[a, :, cols] = sums[a]

    send_first(1)
    send_first(0)
    loads[0].wait()
    loads[1].wait()
    project(1, 0)
    for i in range(1, n):
        forward(1, i)
        project(1, i)
    loads[2].wait()
    loads[3].wait()
    forward(0, 1)
    project(0, 0)
    scale(1)
    if n > 2:
        forward(0, 2)
    gradient(0)
    project(0, 1)
    for i in range(2, n):
        if i > 2:
            forward(0, i)
        project(0, i)
    for slot, job in enumerate((first_job, second_job)):
        for shard in range(n):
            base = slot * rank_full + shard * slots_here
            flat_b[base:base + slots_here, :] = all_b[shard, job]
    scale(0)
    gradient(1)

    @pl.loop(0, count // TILE)
    def _(tile):
        rows = pl.ds(pl.multiple_of(tile * TILE, TILE), TILE)
        adapted[rows, :] = lax.dot_general(
            spread[0, :, rows], flat_b[...], TN, preferred_element_type=jnp.float32).astype(jnp.bfloat16)

    collect(0)
    collect(1)
    for which in range(2):
        finish_sends(which)
        for shard in range(n):
            for step in range(1, mps):
                mp_copy(which, shard, step).wait_send()
        for step in range(1, team):
            rs_copy(which, step).wait_send()


def fits(mesh, tokens, cotangent, adapter_a, adapter_b):
    n, pipes = mesh.shape["dp"], mesh.shape["pipe"]
    slots = adapter_a.shape[1]
    aligned = all(w % TILE == 0 for w in (tokens.shape[0], tokens.shape[1], cotangent.shape[1]))
    return pipes == 2 and n >= 2 and n <= 8 and slots % (ROWS16 * pipes) == 0 and adapter_a.shape[0] % 2 == 0 and aligned


def one_kernel(mesh, tokens, cotangent, tok_job, job_list, job_rank, adapter_a, adapter_b):
    n, pipes, mps = mesh.shape["dp"], mesh.shape["pipe"], mesh.shape["mp"]
    adapters, slots, width_a = adapter_a.shape
    width_b = adapter_b.shape[2]
    count = tokens.shape[0]
    team = n * pipes
    each = slots // pipes
    bf16, f32 = jnp.bfloat16, jnp.float32
    anywhere = pl.BlockSpec(memory_space=pl.ANY)
    vmem = pl.BlockSpec(memory_space=pltpu.VMEM)
    smem = pl.BlockSpec(memory_space=pltpu.SMEM)
    dma = pltpu.SemaphoreType.DMA
    return pl.pallas_call(
        functools.partial(fused, n, pipes, mps),
        out_shape=(
            jax.ShapeDtypeStruct((count, width_b), bf16),
            jax.ShapeDtypeStruct((adapters, each, width_a), f32),
            jax.ShapeDtypeStruct((adapters, each, width_b), f32),
        ),
        in_specs=[anywhere, anywhere, vmem, smem, smem, anywhere, anywhere],
        out_specs=(vmem, vmem, vmem),
        scratch_shapes=[
            pltpu.VMEM((count, width_a), bf16),
            pltpu.VMEM((count, width_b), bf16),
            pltpu.VMEM((n, adapters, slots, width_a), bf16),
            pltpu.VMEM((n, adapters, slots, width_b), bf16),
            pltpu.VMEM((2, n, slots, count), f32),
            pltpu.VMEM((2, n, slots, count), bf16),
            pltpu.VMEM((2, mps, n, slots, count), bf16),
            pltpu.VMEM((2, 2 * n * slots, count), bf16),
            pltpu.VMEM((2 * n * slots, width_b), bf16),
            pltpu.VMEM((team, 2, each, width_a), bf16),
            pltpu.VMEM((team, 2, each, width_b), bf16),
            pltpu.VMEM((team, 2, each, width_a), bf16),
            pltpu.VMEM((team, 2, each, width_b), bf16),
            dma((4,)),
            dma((2, n)), dma((2, n)), dma((2, n)), dma((2, n)), dma((2, n)),
            dma((2, n, mps)), dma((2, mps, n)),
            dma((2, team)), dma((2, team)),
        ],
        compiler_params=pltpu.CompilerParams(
            collective_id=0, has_side_effects=True, vmem_limit_bytes=48 * 1024 * 1024),
        cost_estimate=pl.CostEstimate(
            flops=2 * count * 8 * n * slots * (width_a + width_b), bytes_accessed=12 * 1024 * 1024, transcendentals=0),
    )(tokens, cotangent, tok_job.reshape(1, count), job_list, job_rank, adapter_a, adapter_b)


def on_device_plain(tokens, cotangent, tok_job, job_list, job_rank, adapter_a, adapter_b):
    high = lax.Precision.HIGHEST
    here = lax.axis_index("dp")
    layer = lax.axis_index("pipe")
    count_dp = lax.axis_size("dp")
    rank_full = adapter_a.shape[1] * count_dp
    slots = job_list.shape[2]
    adapters = adapter_a.shape[0]
    width_a = adapter_a.shape[2]
    width_b = adapter_b.shape[2]
    count = tokens.shape[0]
    peer_jobs = lax.dynamic_index_in_dim(job_list, layer, 1, keepdims=False)
    own_jobs = lax.dynamic_index_in_dim(peer_jobs, here, 0, keepdims=False)
    whole_a, whole_b = (
        lax.all_gather(adapter_a, "dp", axis=1, tiled=True),
        lax.all_gather(adapter_b, "dp", axis=1, tiled=True),
    )
    tiles_a = whole_a[own_jobs]
    tiles_b = whole_b[own_jobs]
    onehot = (tok_job[:, None] == own_jobs[None, :]).astype(jnp.float32)
    slot_ranks = job_rank[own_jobs]
    levels = lax.broadcasted_iota(jnp.int32, (slots, rank_full), 1)
    slot_mask = (levels < slot_ranks[:, None]).astype(jnp.float32)
    slot_scale = 8.0 / jnp.sqrt(slot_ranks.astype(jnp.float32))
    tok_mask = jnp.dot(onehot, slot_mask, precision=high)
    tok_scale = jnp.dot(onehot, slot_scale, precision=high)
    flat_a = tiles_a.reshape(slots * rank_full, width_a)
    flat_b = tiles_b.reshape(slots * rank_full, width_b)
    low_all = jnp.einsum("td,kd->tk", tokens, flat_a, preferred_element_type=jnp.float32)
    back_all = jnp.einsum("to,ko->tk", cotangent, flat_b, preferred_element_type=jnp.float32)
    low_part = jnp.sum(onehot[:, :, None] * low_all.reshape(count, slots, rank_full), axis=1)
    back_part = jnp.sum(onehot[:, :, None] * back_all.reshape(count, slots, rank_full), axis=1)
    low, back = lax.psum((low_part, back_part), "mp")
    scaled_low = (low * tok_mask * tok_scale[:, None]).astype(jnp.bfloat16)
    scaled_back = (back * tok_mask * tok_scale[:, None]).astype(jnp.bfloat16)
    picker = onehot.astype(jnp.bfloat16)[:, :, None]
    spread_low = (picker * scaled_low[:, None, :]).reshape(count, slots * rank_full)
    spread_back = (picker * scaled_back[:, None, :]).reshape(count, slots * rank_full)
    adapted = jnp.dot(spread_low, flat_b, preferred_element_type=jnp.float32).astype(jnp.bfloat16)
    part_b = jnp.einsum("tk,to->ko", spread_low, cotangent, preferred_element_type=jnp.float32)
    part_a = jnp.einsum("tk,td->kd", spread_back, tokens, preferred_element_type=jnp.float32)
    part_b = part_b.reshape(slots, rank_full, width_b)
    part_a = part_a.reshape(slots, rank_full, width_a)
    everyone = lax.broadcasted_iota(jnp.int32, (1, adapters), 1)
    select = (own_jobs[:, None] == everyone).astype(jnp.float32)
    dense_a = jnp.einsum("ja,jrd->ard", select, part_a, precision=high)
    dense_b = jnp.einsum("ja,jro->aro", select, part_b, precision=high)
    grad_a, grad_b = (
        lax.psum_scatter(dense_a, ("dp", "pipe"), scatter_dimension=1, tiled=True),
        lax.psum_scatter(dense_b, ("dp", "pipe"), scatter_dimension=1, tiled=True),
    )
    return (adapted, grad_a, grad_b)


def solution(mesh):
    in_specs = (
        P(("groups", "dp", "pipe"), "mp"),
        P(("groups", "dp", "pipe"), "mp"),
        P(("groups", "dp", "pipe")),
        P("groups", None, None),
        P("groups"),
        P("groups", "dp", "mp"),
        P("groups", "dp", "mp"),
    )
    out_specs = (
        P(("groups", "dp", "pipe"), "mp"),
        P("groups", ("dp", "pipe"), "mp"),
        P("groups", ("dp", "pipe"), "mp"),
    )
    def on_device(tokens, cotangent, tok_job, job_list, job_rank, adapter_a, adapter_b):
        args = (tokens, cotangent, tok_job, job_list, job_rank, adapter_a, adapter_b)
        if fits(mesh, tokens, cotangent, adapter_a, adapter_b):
            return one_kernel(mesh, *args)
        return on_device_plain(*args)

    return jax.shard_map(
        on_device, mesh=mesh, in_specs=in_specs, out_specs=out_specs, check_vma=False
    )
```

```python
import functools

import jax
import jax.numpy as jnp
from jax import lax
from jax.experimental import pallas as pl
from jax.experimental.pallas import tpu as pltpu
from jax.sharding import PartitionSpec as P

TILE = 256
ROWS16 = 16
MESH = pl.DeviceIdType.MESH
NT = (((1,), (1,)), ((), ()))
TN = (((0,), (0,)), ((), ()))


def fused(n, pipes, mps,
          tokens_hbm, cot_hbm, job_ref, list_ref, rank_ref, a_hbm, b_hbm,
          adapted, grad_a, grad_b,
          tokens, cot, all_a, all_b, own, away, here_mp, spread, flat_b,
          part_a, part_b, got_a, got_b, mid_a, mid_b, dense_a, dense_b, far_a, far_b,
          local_sem, right_sem, left_sem, line_sem, sib_send, sib_recv,
          mp_send, mp_recv, rs_send, rs_recv, mid_recv, far_send, far_recv):
    z = lax.axis_index("dp")
    core = lax.axis_index("pipe")
    lane = lax.axis_index("mp")
    me = z * pipes + core
    adapters, slots_here = a_hbm.shape[0], a_hbm.shape[1]
    count = tokens.shape[0]
    rank_full = n * slots_here
    half = adapters // pipes
    team = n * pipes

    loads = [
        pltpu.make_async_copy(b_hbm, all_b.at[z], local_sem.at[0]),
        pltpu.make_async_copy(cot_hbm, cot, local_sem.at[1]),
        pltpu.make_async_copy(a_hbm, all_a.at[z], local_sem.at[2]),
        pltpu.make_async_copy(tokens_hbm, tokens, local_sem.at[3]),
    ]
    for load in loads:
        load.start()

    barrier = pltpu.get_barrier_semaphore()
    for step in range(1, team):
        peer = lax.rem(me + step, team)
        pl.semaphore_signal(barrier, inc=1, device_id={"dp": peer // pipes, "pipe": lax.rem(peer, pipes)}, device_id_type=MESH)
    for step in range(1, mps):
        pl.semaphore_signal(barrier, inc=1, device_id={"mp": lax.rem(lane + step, mps)}, device_id_type=MESH)
    pl.semaphore_wait(barrier, team - 1 + mps - 1)

    stores = (all_a, all_b)
    sources = (a_hbm, b_hbm)

    def part_of(ref, c):
        return ref.at[pl.ds(c * half, half)]

    def line_copy(which, shard, rightward, first):
        held = stores[which]
        src = part_of(sources[which], core) if first else part_of(held.at[shard], core)
        sem = right_sem if rightward else left_sem
        return pltpu.make_async_remote_copy(
            src_ref=src, dst_ref=part_of(held.at[shard], core),
            send_sem=sem.at[which, shard], recv_sem=line_sem.at[which, shard],
            device_id={"dp": z + 1 if rightward else z - 1}, device_id_type=MESH)

    def sib_copy(which, shard, c):
        held = stores[which]
        return pltpu.make_async_remote_copy(
            src_ref=part_of(held.at[shard], c), dst_ref=part_of(held.at[shard], c),
            send_sem=sib_send.at[which, shard], recv_sem=sib_recv.at[which, shard],
            device_id={"pipe": 1 - core}, device_id_type=MESH)

    near = jnp.minimum(z, n - 1 - z)

    def shard_at(i):
        if i == 0:
            return z
        paired = z - (i + 1) // 2 if i % 2 else z + i // 2
        return jnp.where(i <= 2 * near, paired, jnp.where(z < n - 1 - z, i, n - 1 - i))

    def send_first(which):
        @pl.when(z < n - 1)
        def _():
            line_copy(which, z, True, True).start()

        @pl.when(z > 0)
        def _():
            line_copy(which, z, False, True).start()

    def forward(which, i):
        shard = shard_at(i)
        line_copy(which, shard, True, False).wait_recv()

        @pl.when(jnp.logical_and(shard < z, z < n - 1))
        def _():
            line_copy(which, shard, True, False).start()

        @pl.when(jnp.logical_and(shard > z, z > 0))
        def _():
            line_copy(which, shard, False, False).start()

        sib_copy(which, shard, core).start()

    def finish_sends(which):
        for i in range(n):
            shard = shard_at(i)

            @pl.when(jnp.logical_and(shard <= z, z < n - 1))
            def _():
                line_copy(which, shard, True, i == 0).wait_send()

            @pl.when(jnp.logical_and(shard >= z, z > 0))
            def _():
                line_copy(which, shard, False, i == 0).wait_send()

            if i > 0:
                sib_copy(which, shard, core).wait_send()

    def mp_copy(which, shard, step):
        return pltpu.make_async_remote_copy(
            src_ref=away.at[which, shard], dst_ref=here_mp.at[which, lane, shard],
            send_sem=mp_send.at[which, shard, step], recv_sem=mp_recv.at[which, lane, shard],
            device_id={"mp": lax.rem(lane + step, mps)}, device_id_type=MESH)

    def mp_arrived(which, shard, step):
        peer = lax.rem(lane + step, mps)
        return pltpu.make_async_remote_copy(
            src_ref=away.at[which, shard], dst_ref=here_mp.at[which, peer, shard],
            send_sem=mp_send.at[which, shard, step], recv_sem=mp_recv.at[which, peer, shard],
            device_id={"mp": peer}, device_id_type=MESH)

    def project(which, i):
        shard = shard_at(i)
        held = stores[which]
        rows = tokens if which == 0 else cot
        if i > 0:
            sib_copy(which, shard, 1 - core).wait_recv()
        factor = held[shard].reshape(adapters * slots_here, held.shape[3])

        @pl.loop(0, count // TILE)
        def _(tile):
            cols = pl.ds(pl.multiple_of(tile * TILE, TILE), TILE)
            got = lax.dot_general(factor, rows[cols, :], NT, preferred_element_type=jnp.float32)
            jobs = job_ref[:, cols]
            value = jnp.zeros((slots_here, TILE), jnp.float32)
            for a in range(adapters):
                value = jnp.where(jobs == a, got[a * slots_here:(a + 1) * slots_here], value)
            own[which, shard, :, cols] = value
            away[which, shard, :, cols] = value.astype(jnp.bfloat16)

        for step in range(1, mps):
            mp_copy(which, shard, step).start()

    first_job = list_ref[z, core, 0]
    second_job = list_ref[z, core, 1]

    def scale(which):
        jobs = job_ref[...]
        ranks = jnp.zeros_like(jobs)
        for a in range(adapters):
            ranks = jnp.where(jobs == a, rank_ref[a], ranks)
        gain = 8.0 / jnp.sqrt(ranks.astype(jnp.float32))
        for shard in range(n):
            value = own[which, shard]
            for step in range(1, mps):
                mp_arrived(which, shard, step).wait_recv()
                value = value + here_mp[which, lax.rem(lane + step, mps), shard].astype(jnp.float32)
            level = lax.broadcasted_iota(jnp.int32, value.shape, 0) + shard * slots_here
            value = jnp.where(level < ranks, value * gain, 0.0)
            base = shard * slots_here
            spread[which, base:base + slots_here, :] = jnp.where(jobs == first_job, value, 0.0).astype(jnp.bfloat16)
            base += rank_full
            spread[which, base:base + slots_here, :] = jnp.where(jobs == second_job, value, 0.0).astype(jnp.bfloat16)

    bridge = jnp.where(z < n // 2, n // 2 - 1, n // 2)
    base_z = jnp.where(z < n // 2, 0, n // 2)
    far_z = n // 2 - base_z
    side = team // 2
    spot = me - base_z * pipes

    def parts_of(which):
        return ((part_a, got_a, mid_a, dense_a, far_a), (part_b, got_b, mid_b, dense_b, far_b))[which]

    def near_copy(which, source, target):
        part, got = parts_of(which)[:2]
        dest = base_z * pipes + target
        return pltpu.make_async_remote_copy(
            src_ref=part.at[dest], dst_ref=got.at[source],
            send_sem=rs_send.at[which, dest], recv_sem=rs_recv.at[which, source],
            device_id={"dp": dest // pipes, "pipe": lax.rem(dest, pipes)}, device_id_type=MESH)

    def bridge_copy(which, source, far, c):
        part, mid = parts_of(which)[0], parts_of(which)[2]
        dest = (far_z + far) * pipes + c
        return pltpu.make_async_remote_copy(
            src_ref=part.at[dest], dst_ref=mid.at[source, far],
            send_sem=rs_send.at[which, dest], recv_sem=mid_recv.at[which, source, far],
            device_id={"dp": bridge, "pipe": c}, device_id_type=MESH)

    def far_copy(which, far):
        dense, landed = parts_of(which)[3:]
        return pltpu.make_async_remote_copy(
            src_ref=dense.at[far], dst_ref=landed,
            send_sem=far_send.at[which, far], recv_sem=far_recv.at[which],
            device_id={"dp": far_z + far}, device_id_type=MESH)

    def each_bridge_send(which, act):
        for far in range(n // 2):
            for c in range(pipes):
                @pl.when(jnp.logical_or(z != bridge, core != c))
                def _():
                    act(bridge_copy(which, spot, far, c))

    def added(which, term_of, cols):
        sums = [None] * adapters
        for source in range(side):
            for slot in range(2):
                job = list_ref[base_z + source // pipes, source % pipes, slot]
                term = term_of(source, slot, cols).astype(jnp.float32)
                for a in range(adapters):
                    piece = term * jnp.where(job == a, 1.0, 0.0)
                    sums[a] = piece if sums[a] is None else sums[a] + piece
        return sums

    def combine(which):
        part, _, mid, dense, _ = parts_of(which)

        @pl.when(z == bridge)
        def _():
            for far in range(n // 2):
                mid[spot, far] = part[(far_z + far) * pipes + core]
                for step in range(1, side):
                    bridge_copy(which, lax.rem(spot + step, side), far, core).wait_recv()

                @pl.loop(0, dense.shape[3] // TILE)
                def _(tile):
                    cols = pl.ds(pl.multiple_of(tile * TILE, TILE), TILE)
                    sums = added(which, lambda source, slot, cols: mid[source, far, slot, :, cols], cols)
                    for a in range(adapters):
                        dense[far, a, :, cols] = sums[a].astype(jnp.bfloat16)

                far_copy(which, far).start()

    def gradient(which):
        rows = tokens if which == 0 else cot
        part, got = parts_of(which)[:2]
        weights = spread[1 - which]
        each = rank_full // team

        @pl.loop(0, rows.shape[1] // TILE)
        def _(tile):
            cols = pl.ds(pl.multiple_of(tile * TILE, TILE), TILE)
            out = jnp.dot(weights, rows[:, cols], preferred_element_type=jnp.float32).astype(jnp.bfloat16)
            for dest in range(team):
                for slot in range(2):
                    base = slot * rank_full + dest * each
                    part[dest, slot, :, cols] = out[base:base + each]

        each_bridge_send(which, lambda copy: copy.start())
        for step in range(1, side):
            near_copy(which, spot, lax.rem(spot + step, side)).start()
        got[spot] = part[me]

    def collect(which):
        got, landed = parts_of(which)[1], parts_of(which)[4]
        out = (grad_a, grad_b)[which]
        for step in range(1, side):
            near_copy(which, lax.rem(spot + step, side), spot).wait_recv()
        far_copy(which, 0).wait_recv()

        @pl.loop(0, out.shape[2] // TILE)
        def _(tile):
            cols = pl.ds(pl.multiple_of(tile * TILE, TILE), TILE)
            sums = added(which, lambda source, slot, cols: got[source, slot, :, cols], cols)
            for a in range(adapters):
                out[a, :, cols] = sums[a] + landed[a, :, cols].astype(jnp.float32)

    send_first(1)
    send_first(0)
    loads[0].wait()
    loads[1].wait()
    project(1, 0)
    for i in range(1, n):
        forward(1, i)
        project(1, i)
    loads[2].wait()
    loads[3].wait()
    forward(0, 1)
    project(0, 0)
    scale(1)
    if n > 2:
        forward(0, 2)
    gradient(0)
    project(0, 1)
    for i in range(2, n):
        if i > 2:
            forward(0, i)
        project(0, i)
    for slot, job in enumerate((first_job, second_job)):
        for shard in range(n):
            base = slot * rank_full + shard * slots_here
            flat_b[base:base + slots_here, :] = all_b[shard, job]
    scale(0)
    gradient(1)
    combine(0)

    @pl.loop(0, count // TILE)
    def _(tile):
        rows = pl.ds(pl.multiple_of(tile * TILE, TILE), TILE)
        adapted[rows, :] = lax.dot_general(
            spread[0, :, rows], flat_b[...], TN, preferred_element_type=jnp.float32).astype(jnp.bfloat16)

    combine(1)
    collect(0)
    collect(1)
    for which in range(2):
        finish_sends(which)
        for shard in range(n):
            for step in range(1, mps):
                mp_copy(which, shard, step).wait_send()
        each_bridge_send(which, lambda copy: copy.wait_send())
        for step in range(1, side):
            near_copy(which, spot, lax.rem(spot + step, side)).wait_send()

        @pl.when(z == bridge)
        def _():
            for far in range(n // 2):
                far_copy(which, far).wait_send()


def fits(mesh, tokens, cotangent, adapter_a, adapter_b):
    n, pipes = mesh.shape["dp"], mesh.shape["pipe"]
    slots = adapter_a.shape[1]
    aligned = all(w % TILE == 0 for w in (tokens.shape[0], tokens.shape[1], cotangent.shape[1]))
    return pipes == 2 and n >= 2 and n <= 8 and n % 2 == 0 and slots % (ROWS16 * pipes) == 0 and adapter_a.shape[0] % 2 == 0 and aligned


def one_kernel(mesh, tokens, cotangent, tok_job, job_list, job_rank, adapter_a, adapter_b):
    n, pipes, mps = mesh.shape["dp"], mesh.shape["pipe"], mesh.shape["mp"]
    adapters, slots, width_a = adapter_a.shape
    width_b = adapter_b.shape[2]
    count = tokens.shape[0]
    team = n * pipes
    each = slots // pipes
    bf16, f32 = jnp.bfloat16, jnp.float32
    anywhere = pl.BlockSpec(memory_space=pl.ANY)
    vmem = pl.BlockSpec(memory_space=pltpu.VMEM)
    smem = pl.BlockSpec(memory_space=pltpu.SMEM)
    dma = pltpu.SemaphoreType.DMA
    return pl.pallas_call(
        functools.partial(fused, n, pipes, mps),
        out_shape=(
            jax.ShapeDtypeStruct((count, width_b), bf16),
            jax.ShapeDtypeStruct((adapters, each, width_a), f32),
            jax.ShapeDtypeStruct((adapters, each, width_b), f32),
        ),
        in_specs=[anywhere, anywhere, vmem, smem, smem, anywhere, anywhere],
        out_specs=(vmem, vmem, vmem),
        scratch_shapes=[
            pltpu.VMEM((count, width_a), bf16),
            pltpu.VMEM((count, width_b), bf16),
            pltpu.VMEM((n, adapters, slots, width_a), bf16),
            pltpu.VMEM((n, adapters, slots, width_b), bf16),
            pltpu.VMEM((2, n, slots, count), f32),
            pltpu.VMEM((2, n, slots, count), bf16),
            pltpu.VMEM((2, mps, n, slots, count), bf16),
            pltpu.VMEM((2, 2 * n * slots, count), bf16),
            pltpu.VMEM((2 * n * slots, width_b), bf16),
            pltpu.VMEM((team, 2, each, width_a), bf16),
            pltpu.VMEM((team, 2, each, width_b), bf16),
            pltpu.VMEM((team // 2, 2, each, width_a), bf16),
            pltpu.VMEM((team // 2, 2, each, width_b), bf16),
            pltpu.VMEM((team // 2, n // 2, 2, each, width_a), bf16),
            pltpu.VMEM((team // 2, n // 2, 2, each, width_b), bf16),
            pltpu.VMEM((n // 2, adapters, each, width_a), bf16),
            pltpu.VMEM((n // 2, adapters, each, width_b), bf16),
            pltpu.VMEM((adapters, each, width_a), bf16),
            pltpu.VMEM((adapters, each, width_b), bf16),
            dma((4,)),
            dma((2, n)), dma((2, n)), dma((2, n)), dma((2, n)), dma((2, n)),
            dma((2, n, mps)), dma((2, mps, n)),
            dma((2, team)), dma((2, team // 2)),
            dma((2, team // 2, n // 2)), dma((2, n // 2)), dma((2,)),
        ],
        compiler_params=pltpu.CompilerParams(
            collective_id=0, has_side_effects=True, vmem_limit_bytes=60 * 1024 * 1024),
        cost_estimate=pl.CostEstimate(
            flops=2 * count * 8 * n * slots * (width_a + width_b), bytes_accessed=12 * 1024 * 1024, transcendentals=0),
    )(tokens, cotangent, tok_job.reshape(1, count), job_list, job_rank, adapter_a, adapter_b)


def on_device_plain(tokens, cotangent, tok_job, job_list, job_rank, adapter_a, adapter_b):
    high = lax.Precision.HIGHEST
    here = lax.axis_index("dp")
    layer = lax.axis_index("pipe")
    count_dp = lax.axis_size("dp")
    rank_full = adapter_a.shape[1] * count_dp
    slots = job_list.shape[2]
    adapters = adapter_a.shape[0]
    width_a = adapter_a.shape[2]
    width_b = adapter_b.shape[2]
    count = tokens.shape[0]
    peer_jobs = lax.dynamic_index_in_dim(job_list, layer, 1, keepdims=False)
    own_jobs = lax.dynamic_index_in_dim(peer_jobs, here, 0, keepdims=False)
    whole_a, whole_b = (
        lax.all_gather(adapter_a, "dp", axis=1, tiled=True),
        lax.all_gather(adapter_b, "dp", axis=1, tiled=True),
    )
    tiles_a = whole_a[own_jobs]
    tiles_b = whole_b[own_jobs]
    onehot = (tok_job[:, None] == own_jobs[None, :]).astype(jnp.float32)
    slot_ranks = job_rank[own_jobs]
    levels = lax.broadcasted_iota(jnp.int32, (slots, rank_full), 1)
    slot_mask = (levels < slot_ranks[:, None]).astype(jnp.float32)
    slot_scale = 8.0 / jnp.sqrt(slot_ranks.astype(jnp.float32))
    tok_mask = jnp.dot(onehot, slot_mask, precision=high)
    tok_scale = jnp.dot(onehot, slot_scale, precision=high)
    flat_a = tiles_a.reshape(slots * rank_full, width_a)
    flat_b = tiles_b.reshape(slots * rank_full, width_b)
    low_all = jnp.einsum("td,kd->tk", tokens, flat_a, preferred_element_type=jnp.float32)
    back_all = jnp.einsum("to,ko->tk", cotangent, flat_b, preferred_element_type=jnp.float32)
    low_part = jnp.sum(onehot[:, :, None] * low_all.reshape(count, slots, rank_full), axis=1)
    back_part = jnp.sum(onehot[:, :, None] * back_all.reshape(count, slots, rank_full), axis=1)
    low, back = lax.psum((low_part, back_part), "mp")
    scaled_low = (low * tok_mask * tok_scale[:, None]).astype(jnp.bfloat16)
    scaled_back = (back * tok_mask * tok_scale[:, None]).astype(jnp.bfloat16)
    picker = onehot.astype(jnp.bfloat16)[:, :, None]
    spread_low = (picker * scaled_low[:, None, :]).reshape(count, slots * rank_full)
    spread_back = (picker * scaled_back[:, None, :]).reshape(count, slots * rank_full)
    adapted = jnp.dot(spread_low, flat_b, preferred_element_type=jnp.float32).astype(jnp.bfloat16)
    part_b = jnp.einsum("tk,to->ko", spread_low, cotangent, preferred_element_type=jnp.float32)
    part_a = jnp.einsum("tk,td->kd", spread_back, tokens, preferred_element_type=jnp.float32)
    part_b = part_b.reshape(slots, rank_full, width_b)
    part_a = part_a.reshape(slots, rank_full, width_a)
    everyone = lax.broadcasted_iota(jnp.int32, (1, adapters), 1)
    select = (own_jobs[:, None] == everyone).astype(jnp.float32)
    dense_a = jnp.einsum("ja,jrd->ard", select, part_a, precision=high)
    dense_b = jnp.einsum("ja,jro->aro", select, part_b, precision=high)
    grad_a, grad_b = (
        lax.psum_scatter(dense_a, ("dp", "pipe"), scatter_dimension=1, tiled=True),
        lax.psum_scatter(dense_b, ("dp", "pipe"), scatter_dimension=1, tiled=True),
    )
    return (adapted, grad_a, grad_b)


def solution(mesh):
    in_specs = (
        P(("groups", "dp", "pipe"), "mp"),
        P(("groups", "dp", "pipe"), "mp"),
        P(("groups", "dp", "pipe")),
        P("groups", None, None),
        P("groups"),
        P("groups", "dp", "mp"),
        P("groups", "dp", "mp"),
    )
    out_specs = (
        P(("groups", "dp", "pipe"), "mp"),
        P("groups", ("dp", "pipe"), "mp"),
        P("groups", ("dp", "pipe"), "mp"),
    )
    def on_device(tokens, cotangent, tok_job, job_list, job_rank, adapter_a, adapter_b):
        args = (tokens, cotangent, tok_job, job_list, job_rank, adapter_a, adapter_b)
        if fits(mesh, tokens, cotangent, adapter_a, adapter_b):
            return one_kernel(mesh, *args)
        return on_device_plain(*args)

    return jax.shard_map(
        on_device, mesh=mesh, in_specs=in_specs, out_specs=out_specs, check_vma=False
    )
```

```python
import functools

import jax
import jax.numpy as jnp
from jax import lax
from jax.experimental import pallas as pl
from jax.experimental.pallas import tpu as pltpu
from jax.sharding import PartitionSpec as P

TILE = 256
ROWS16 = 16
MESH = pl.DeviceIdType.MESH
NT = (((1,), (1,)), ((), ()))
TN = (((0,), (0,)), ((), ()))


def fused(n, pipes, mps,
          tokens_hbm, cot_hbm, job_ref, list_ref, rank_ref, a_hbm, b_hbm,
          adapted, grad_a, grad_b,
          tokens, cot, all_a, all_b, own, away, here_mp, spread, flat_b,
          part_a, part_b, got_a, got_b, mid_a, mid_b, dense_a, dense_b, far_a, far_b,
          local_sem, right_sem, left_sem, line_sem, sib_send, sib_recv,
          mp_send, mp_recv, rs_send, rs_recv, mid_recv, far_send, far_recv):
    z = lax.axis_index("dp")
    core = lax.axis_index("pipe")
    lane = lax.axis_index("mp")
    me = z * pipes + core
    adapters, slots_here = a_hbm.shape[0], a_hbm.shape[1]
    count = tokens.shape[0]
    rank_full = n * slots_here
    half = adapters // pipes
    team = n * pipes

    loads = [
        pltpu.make_async_copy(b_hbm, all_b.at[z], local_sem.at[0]),
        pltpu.make_async_copy(cot_hbm, cot, local_sem.at[1]),
        pltpu.make_async_copy(a_hbm, all_a.at[z], local_sem.at[2]),
        pltpu.make_async_copy(tokens_hbm, tokens, local_sem.at[3]),
    ]
    for load in loads:
        load.start()

    barrier = pltpu.get_barrier_semaphore()
    for step in range(1, team):
        peer = lax.rem(me + step, team)
        pl.semaphore_signal(barrier, inc=1, device_id={"dp": peer // pipes, "pipe": lax.rem(peer, pipes)}, device_id_type=MESH)
    for step in range(1, mps):
        pl.semaphore_signal(barrier, inc=1, device_id={"mp": lax.rem(lane + step, mps)}, device_id_type=MESH)
    pl.semaphore_wait(barrier, team - 1 + mps - 1)

    stores = (all_a, all_b)
    sources = (a_hbm, b_hbm)

    def part_of(ref, c):
        return ref.at[pl.ds(c * half, half)]

    def line_copy(which, shard, rightward, first):
        held = stores[which]
        src = part_of(sources[which], core) if first else part_of(held.at[shard], core)
        sem = right_sem if rightward else left_sem
        return pltpu.make_async_remote_copy(
            src_ref=src, dst_ref=part_of(held.at[shard], core),
            send_sem=sem.at[which, shard], recv_sem=line_sem.at[which, shard],
            device_id={"dp": z + 1 if rightward else z - 1}, device_id_type=MESH)

    def sib_copy(which, shard, c):
        held = stores[which]
        return pltpu.make_async_remote_copy(
            src_ref=part_of(held.at[shard], c), dst_ref=part_of(held.at[shard], c),
            send_sem=sib_send.at[which, shard], recv_sem=sib_recv.at[which, shard],
            device_id={"pipe": 1 - core}, device_id_type=MESH)

    near = jnp.minimum(z, n - 1 - z)

    def shard_at(i):
        if i == 0:
            return z
        paired = z - (i + 1) // 2 if i % 2 else z + i // 2
        return jnp.where(i <= 2 * near, paired, jnp.where(z < n - 1 - z, i, n - 1 - i))

    def send_first(which):
        @pl.when(z < n - 1)
        def _():
            line_copy(which, z, True, True).start()

        @pl.when(z > 0)
        def _():
            line_copy(which, z, False, True).start()

    def forward(which, i):
        shard = shard_at(i)
        line_copy(which, shard, True, False).wait_recv()

        @pl.when(jnp.logical_and(shard < z, z < n - 1))
        def _():
            line_copy(which, shard, True, False).start()

        @pl.when(jnp.logical_and(shard > z, z > 0))
        def _():
            line_copy(which, shard, False, False).start()

        sib_copy(which, shard, core).start()

    def finish_sends(which):
        for i in range(n):
            shard = shard_at(i)

            @pl.when(jnp.logical_and(shard <= z, z < n - 1))
            def _():
                line_copy(which, shard, True, i == 0).wait_send()

            @pl.when(jnp.logical_and(shard >= z, z > 0))
            def _():
                line_copy(which, shard, False, i == 0).wait_send()

            if i > 0:
                sib_copy(which, shard, core).wait_send()

    def mp_copy(which, shard, step):
        return pltpu.make_async_remote_copy(
            src_ref=away.at[which, shard], dst_ref=here_mp.at[which, lane, shard],
            send_sem=mp_send.at[which, shard, step], recv_sem=mp_recv.at[which, lane, shard],
            device_id={"mp": lax.rem(lane + step, mps)}, device_id_type=MESH)

    def mp_arrived(which, shard, step):
        peer = lax.rem(lane + step, mps)
        return pltpu.make_async_remote_copy(
            src_ref=away.at[which, shard], dst_ref=here_mp.at[which, peer, shard],
            send_sem=mp_send.at[which, shard, step], recv_sem=mp_recv.at[which, peer, shard],
            device_id={"mp": peer}, device_id_type=MESH)

    def project(which, i):
        shard = shard_at(i)
        held = stores[which]
        rows = tokens if which == 0 else cot
        if i > 0:
            sib_copy(which, shard, 1 - core).wait_recv()
        factor = held[shard].reshape(adapters * slots_here, held.shape[3])

        @pl.loop(0, count // 512)
        def _(tile):
            cols = pl.ds(pl.multiple_of(tile * 512, 512), 512)
            got = lax.dot_general(factor, rows[cols, :], NT, preferred_element_type=jnp.float32)
            jobs = job_ref[:, cols]
            value = jnp.zeros((slots_here, 512), jnp.float32)
            for a in range(adapters):
                value = jnp.where(jobs == a, got[a * slots_here:(a + 1) * slots_here], value)
            own[which, shard, :, cols] = value
            away[which, shard, :, cols] = value.astype(jnp.bfloat16)

        for step in range(1, mps):
            mp_copy(which, shard, step).start()

    first_job = list_ref[z, core, 0]
    second_job = list_ref[z, core, 1]

    def scale(which):
        jobs = job_ref[...]
        ranks = jnp.zeros_like(jobs)
        for a in range(adapters):
            ranks = jnp.where(jobs == a, rank_ref[a], ranks)
        gain = 8.0 / jnp.sqrt(ranks.astype(jnp.float32))
        for shard in range(n):
            value = own[which, shard]
            for step in range(1, mps):
                mp_arrived(which, shard, step).wait_recv()
                value = value + here_mp[which, lax.rem(lane + step, mps), shard].astype(jnp.float32)
            level = lax.broadcasted_iota(jnp.int32, value.shape, 0) + shard * slots_here
            value = jnp.where(level < ranks, value * gain, 0.0)
            base = shard * slots_here
            spread[which, base:base + slots_here, :] = jnp.where(jobs == first_job, value, 0.0).astype(jnp.bfloat16)
            base += rank_full
            spread[which, base:base + slots_here, :] = jnp.where(jobs == second_job, value, 0.0).astype(jnp.bfloat16)

    bridge = jnp.where(z < n // 2, n // 2 - 1, n // 2)
    base_z = jnp.where(z < n // 2, 0, n // 2)
    far_z = n // 2 - base_z
    side = team // 2
    spot = me - base_z * pipes

    def parts_of(which):
        return ((part_a, got_a, mid_a, dense_a, far_a), (part_b, got_b, mid_b, dense_b, far_b))[which]

    def near_copy(which, source, target):
        part, got = parts_of(which)[:2]
        dest = base_z * pipes + target
        return pltpu.make_async_remote_copy(
            src_ref=part.at[dest], dst_ref=got.at[source],
            send_sem=rs_send.at[which, dest], recv_sem=rs_recv.at[which, source],
            device_id={"dp": dest // pipes, "pipe": lax.rem(dest, pipes)}, device_id_type=MESH)

    def bridge_copy(which, source, far, c):
        part, mid = parts_of(which)[0], parts_of(which)[2]
        dest = (far_z + far) * pipes + c
        return pltpu.make_async_remote_copy(
            src_ref=part.at[dest], dst_ref=mid.at[source, far],
            send_sem=rs_send.at[which, dest], recv_sem=mid_recv.at[which, source, far],
            device_id={"dp": bridge, "pipe": c}, device_id_type=MESH)

    def far_copy(which, far):
        dense, landed = parts_of(which)[3:]
        return pltpu.make_async_remote_copy(
            src_ref=dense.at[far], dst_ref=landed,
            send_sem=far_send.at[which, far], recv_sem=far_recv.at[which],
            device_id={"dp": far_z + far}, device_id_type=MESH)

    def each_bridge_send(which, act):
        for far in range(n // 2):
            for c in range(pipes):
                @pl.when(jnp.logical_or(z != bridge, core != c))
                def _():
                    act(bridge_copy(which, spot, far, c))

    def added(which, term_of, cols):
        sums = [None] * adapters
        for source in range(side):
            for slot in range(2):
                job = list_ref[base_z + source // pipes, source % pipes, slot]
                term = term_of(source, slot, cols).astype(jnp.float32)
                for a in range(adapters):
                    piece = term * jnp.where(job == a, 1.0, 0.0)
                    sums[a] = piece if sums[a] is None else sums[a] + piece
        return sums

    def combine(which):
        part, _, mid, dense, _ = parts_of(which)

        @pl.when(z == bridge)
        def _():
            for far in range(n // 2):
                mid[spot, far] = part[(far_z + far) * pipes + core]
                for step in range(1, side):
                    bridge_copy(which, lax.rem(spot + step, side), far, core).wait_recv()

                @pl.loop(0, dense.shape[3] // TILE)
                def _(tile):
                    cols = pl.ds(pl.multiple_of(tile * TILE, TILE), TILE)
                    sums = added(which, lambda source, slot, cols: mid[source, far, slot, :, cols], cols)
                    for a in range(adapters):
                        dense[far, a, :, cols] = sums[a].astype(jnp.bfloat16)

                far_copy(which, far).start()

    def gradient(which):
        rows = tokens if which == 0 else cot
        part, got = parts_of(which)[:2]
        weights = spread[1 - which]
        each = rank_full // team

        @pl.loop(0, rows.shape[1] // TILE)
        def _(tile):
            cols = pl.ds(pl.multiple_of(tile * TILE, TILE), TILE)
            out = jnp.dot(weights, rows[:, cols], preferred_element_type=jnp.float32).astype(jnp.bfloat16)
            for dest in range(team):
                for slot in range(2):
                    base = slot * rank_full + dest * each
                    part[dest, slot, :, cols] = out[base:base + each]

        each_bridge_send(which, lambda copy: copy.start())
        for step in range(1, side):
            near_copy(which, spot, lax.rem(spot + step, side)).start()
        got[spot] = part[me]

    def collect(which):
        got, landed = parts_of(which)[1], parts_of(which)[4]
        out = (grad_a, grad_b)[which]
        for step in range(1, side):
            near_copy(which, lax.rem(spot + step, side), spot).wait_recv()
        far_copy(which, 0).wait_recv()

        @pl.loop(0, out.shape[2] // TILE)
        def _(tile):
            cols = pl.ds(pl.multiple_of(tile * TILE, TILE), TILE)
            sums = added(which, lambda source, slot, cols: got[source, slot, :, cols], cols)
            for a in range(adapters):
                out[a, :, cols] = sums[a] + landed[a, :, cols].astype(jnp.float32)

    send_first(1)
    send_first(0)
    loads[0].wait()
    loads[1].wait()
    project(1, 0)
    for i in range(1, n):
        forward(1, i)
        project(1, i)
    loads[2].wait()
    loads[3].wait()
    forward(0, 1)
    project(0, 0)
    scale(1)
    if n > 2:
        forward(0, 2)
    gradient(0)
    project(0, 1)
    for i in range(2, n):
        if i > 2:
            forward(0, i)
        project(0, i)
    for slot, job in enumerate((first_job, second_job)):
        for shard in range(n):
            base = slot * rank_full + shard * slots_here
            flat_b[base:base + slots_here, :] = all_b[shard, job]
    scale(0)
    gradient(1)
    combine(0)

    @pl.loop(0, count // TILE)
    def _(tile):
        rows = pl.ds(pl.multiple_of(tile * TILE, TILE), TILE)
        adapted[rows, :] = lax.dot_general(
            spread[0, :, rows], flat_b[...], TN, preferred_element_type=jnp.float32).astype(jnp.bfloat16)

    combine(1)
    collect(0)
    collect(1)
    for which in range(2):
        finish_sends(which)
        for shard in range(n):
            for step in range(1, mps):
                mp_copy(which, shard, step).wait_send()
        each_bridge_send(which, lambda copy: copy.wait_send())
        for step in range(1, side):
            near_copy(which, spot, lax.rem(spot + step, side)).wait_send()

        @pl.when(z == bridge)
        def _():
            for far in range(n // 2):
                far_copy(which, far).wait_send()


def fits(mesh, tokens, cotangent, adapter_a, adapter_b):
    n, pipes = mesh.shape["dp"], mesh.shape["pipe"]
    slots = adapter_a.shape[1]
    aligned = all(w % TILE == 0 for w in (tokens.shape[0], tokens.shape[1], cotangent.shape[1]))
    return pipes == 2 and n >= 2 and n <= 8 and n % 2 == 0 and slots % (ROWS16 * pipes) == 0 and adapter_a.shape[0] % 2 == 0 and aligned


def one_kernel(mesh, tokens, cotangent, tok_job, job_list, job_rank, adapter_a, adapter_b):
    n, pipes, mps = mesh.shape["dp"], mesh.shape["pipe"], mesh.shape["mp"]
    adapters, slots, width_a = adapter_a.shape
    width_b = adapter_b.shape[2]
    count = tokens.shape[0]
    team = n * pipes
    each = slots // pipes
    bf16, f32 = jnp.bfloat16, jnp.float32
    anywhere = pl.BlockSpec(memory_space=pl.ANY)
    vmem = pl.BlockSpec(memory_space=pltpu.VMEM)
    smem = pl.BlockSpec(memory_space=pltpu.SMEM)
    dma = pltpu.SemaphoreType.DMA
    return pl.pallas_call(
        functools.partial(fused, n, pipes, mps),
        out_shape=(
            jax.ShapeDtypeStruct((count, width_b), bf16),
            jax.ShapeDtypeStruct((adapters, each, width_a), f32),
            jax.ShapeDtypeStruct((adapters, each, width_b), f32),
        ),
        in_specs=[anywhere, anywhere, vmem, smem, smem, anywhere, anywhere],
        out_specs=(vmem, vmem, vmem),
        scratch_shapes=[
            pltpu.VMEM((count, width_a), bf16),
            pltpu.VMEM((count, width_b), bf16),
            pltpu.VMEM((n, adapters, slots, width_a), bf16),
            pltpu.VMEM((n, adapters, slots, width_b), bf16),
            pltpu.VMEM((2, n, slots, count), f32),
            pltpu.VMEM((2, n, slots, count), bf16),
            pltpu.VMEM((2, mps, n, slots, count), bf16),
            pltpu.VMEM((2, 2 * n * slots, count), bf16),
            pltpu.VMEM((2 * n * slots, width_b), bf16),
            pltpu.VMEM((team, 2, each, width_a), bf16),
            pltpu.VMEM((team, 2, each, width_b), bf16),
            pltpu.VMEM((team // 2, 2, each, width_a), bf16),
            pltpu.VMEM((team // 2, 2, each, width_b), bf16),
            pltpu.VMEM((team // 2, n // 2, 2, each, width_a), bf16),
            pltpu.VMEM((team // 2, n // 2, 2, each, width_b), bf16),
            pltpu.VMEM((n // 2, adapters, each, width_a), bf16),
            pltpu.VMEM((n // 2, adapters, each, width_b), bf16),
            pltpu.VMEM((adapters, each, width_a), bf16),
            pltpu.VMEM((adapters, each, width_b), bf16),
            dma((4,)),
            dma((2, n)), dma((2, n)), dma((2, n)), dma((2, n)), dma((2, n)),
            dma((2, n, mps)), dma((2, mps, n)),
            dma((2, team)), dma((2, team // 2)),
            dma((2, team // 2, n // 2)), dma((2, n // 2)), dma((2,)),
        ],
        compiler_params=pltpu.CompilerParams(
            collective_id=0, has_side_effects=True, vmem_limit_bytes=60 * 1024 * 1024),
        cost_estimate=pl.CostEstimate(
            flops=2 * count * 8 * n * slots * (width_a + width_b), bytes_accessed=12 * 1024 * 1024, transcendentals=0),
    )(tokens, cotangent, tok_job.reshape(1, count), job_list, job_rank, adapter_a, adapter_b)


def on_device_plain(tokens, cotangent, tok_job, job_list, job_rank, adapter_a, adapter_b):
    high = lax.Precision.HIGHEST
    here = lax.axis_index("dp")
    layer = lax.axis_index("pipe")
    count_dp = lax.axis_size("dp")
    rank_full = adapter_a.shape[1] * count_dp
    slots = job_list.shape[2]
    adapters = adapter_a.shape[0]
    width_a = adapter_a.shape[2]
    width_b = adapter_b.shape[2]
    count = tokens.shape[0]
    peer_jobs = lax.dynamic_index_in_dim(job_list, layer, 1, keepdims=False)
    own_jobs = lax.dynamic_index_in_dim(peer_jobs, here, 0, keepdims=False)
    whole_a, whole_b = (
        lax.all_gather(adapter_a, "dp", axis=1, tiled=True),
        lax.all_gather(adapter_b, "dp", axis=1, tiled=True),
    )
    tiles_a = whole_a[own_jobs]
    tiles_b = whole_b[own_jobs]
    onehot = (tok_job[:, None] == own_jobs[None, :]).astype(jnp.float32)
    slot_ranks = job_rank[own_jobs]
    levels = lax.broadcasted_iota(jnp.int32, (slots, rank_full), 1)
    slot_mask = (levels < slot_ranks[:, None]).astype(jnp.float32)
    slot_scale = 8.0 / jnp.sqrt(slot_ranks.astype(jnp.float32))
    tok_mask = jnp.dot(onehot, slot_mask, precision=high)
    tok_scale = jnp.dot(onehot, slot_scale, precision=high)
    flat_a = tiles_a.reshape(slots * rank_full, width_a)
    flat_b = tiles_b.reshape(slots * rank_full, width_b)
    low_all = jnp.einsum("td,kd->tk", tokens, flat_a, preferred_element_type=jnp.float32)
    back_all = jnp.einsum("to,ko->tk", cotangent, flat_b, preferred_element_type=jnp.float32)
    low_part = jnp.sum(onehot[:, :, None] * low_all.reshape(count, slots, rank_full), axis=1)
    back_part = jnp.sum(onehot[:, :, None] * back_all.reshape(count, slots, rank_full), axis=1)
    low, back = lax.psum((low_part, back_part), "mp")
    scaled_low = (low * tok_mask * tok_scale[:, None]).astype(jnp.bfloat16)
    scaled_back = (back * tok_mask * tok_scale[:, None]).astype(jnp.bfloat16)
    picker = onehot.astype(jnp.bfloat16)[:, :, None]
    spread_low = (picker * scaled_low[:, None, :]).reshape(count, slots * rank_full)
    spread_back = (picker * scaled_back[:, None, :]).reshape(count, slots * rank_full)
    adapted = jnp.dot(spread_low, flat_b, preferred_element_type=jnp.float32).astype(jnp.bfloat16)
    part_b = jnp.einsum("tk,to->ko", spread_low, cotangent, preferred_element_type=jnp.float32)
    part_a = jnp.einsum("tk,td->kd", spread_back, tokens, preferred_element_type=jnp.float32)
    part_b = part_b.reshape(slots, rank_full, width_b)
    part_a = part_a.reshape(slots, rank_full, width_a)
    everyone = lax.broadcasted_iota(jnp.int32, (1, adapters), 1)
    select = (own_jobs[:, None] == everyone).astype(jnp.float32)
    dense_a = jnp.einsum("ja,jrd->ard", select, part_a, precision=high)
    dense_b = jnp.einsum("ja,jro->aro", select, part_b, precision=high)
    grad_a, grad_b = (
        lax.psum_scatter(dense_a, ("dp", "pipe"), scatter_dimension=1, tiled=True),
        lax.psum_scatter(dense_b, ("dp", "pipe"), scatter_dimension=1, tiled=True),
    )
    return (adapted, grad_a, grad_b)


def solution(mesh):
    in_specs = (
        P(("groups", "dp", "pipe"), "mp"),
        P(("groups", "dp", "pipe"), "mp"),
        P(("groups", "dp", "pipe")),
        P("groups", None, None),
        P("groups"),
        P("groups", "dp", "mp"),
        P("groups", "dp", "mp"),
    )
    out_specs = (
        P(("groups", "dp", "pipe"), "mp"),
        P("groups", ("dp", "pipe"), "mp"),
        P("groups", ("dp", "pipe"), "mp"),
    )
    def on_device(tokens, cotangent, tok_job, job_list, job_rank, adapter_a, adapter_b):
        args = (tokens, cotangent, tok_job, job_list, job_rank, adapter_a, adapter_b)
        if fits(mesh, tokens, cotangent, adapter_a, adapter_b):
            return one_kernel(mesh, *args)
        return on_device_plain(*args)

    return jax.shard_map(
        on_device, mesh=mesh, in_specs=in_specs, out_specs=out_specs, check_vma=False
    )
```
